512 devices in a mesh: gx: 64 (over y, z), gy: 8 (over x, core).
Axes of the slice: x: 4, y: 8, z: 8, core: 2. Of those that a mesh axis runs over, the one named last changes fastest.
Arguments:
- load_field: float32 [128, 32, 128, 256], P('gx', 'gy'), may hold values from -6 to 6
- schur_blocks: bfloat16 [128, 32, 256, 256], P('gx', 'gy'), may hold values from -1 to 10, as said below
- local_inverse: bfloat16 [128, 32, 256, 256], P('gx', 'gy'), may hold values from -1 to 10, as said below
- face_order: int32 [128, 32, 2, 64], P('gx', 'gy'), may hold values from 0 to 63, each once within a row
- coarse_weights: float32 [128], replicated, may hold values from 0.03 to 0.12
- coarse_decay: float32 [128, 32], P('gx', 'gy'), may hold values from 0.00390625 to 0.0390625
Outputs:
- solution_field: float32 [128, 32, 128, 256], P('gx', 'gy')
The draws below stay inside these ranges and needn't reach their ends.
Inputs may be any that keep to these rules, and one draw needn't show every extreme that they name: `schur_blocks`: every block is symmetric positive definite. `local_inverse`: every block is symmetric positive definite. `face_order`: each row of 64 numbers holds every number of 0 to 63 once.
All inputs are finite; a program needn't handle non-finite values.
Results may differ from the reference program's by a relative error of at most 0.0022.
Values may be sent and summed in bfloat16 or wider, within the bound.
A program may use at most 64 MiB of HBM per device.

```python
import math
import jax
import jax.numpy as jnp
from jax import lax

FACE = 64
CASES = 256
ITERS = 2
GRID_X = 128
GRID_Y = 32


def draw_schur_blocks(key, part):
    key = jax.random.fold_in(key, 11)
    order_size = 4 * FACE
    block_shape = (GRID_X, GRID_Y, order_size, order_size)
    key_jitter, key_diagonal, key_stiffness = jax.random.split(key, 3)
    spread = 0.3 / order_size ** 0.5
    jitter = jax.random.truncated_normal(key_jitter, -4.0, 4.0, block_shape, jnp.float32)
    diagonal = jax.random.uniform(key_diagonal, block_shape[:3], jnp.float32, 1.0, 2.0)
    stiffness = jnp.exp(jax.random.uniform(key_stiffness, (GRID_X, GRID_Y, 1, 1), jnp.float32, -0.69, 0.69))
    symmetric = (jitter + jnp.swapaxes(jitter, 2, 3)) * (spread * 0.70710678)
    identity = jnp.eye(order_size, dtype=jnp.float32)
    return (stiffness * (symmetric + identity * diagonal[..., None])).astype(jnp.bfloat16)


def draw_local_inverse(key, part):
    key = jax.random.fold_in(key, 23)
    order_size = 4 * FACE
    block_shape = (GRID_X, GRID_Y, order_size, order_size)
    key_jitter, key_diagonal, key_stiffness = jax.random.split(key, 3)
    spread = 0.3 / order_size ** 0.5
    jitter = jax.random.truncated_normal(key_jitter, -4.0, 4.0, block_shape, jnp.float32)
    diagonal = jax.random.uniform(key_diagonal, block_shape[:3], jnp.float32, 1.0, 2.0)
    stiffness = jnp.exp(jax.random.uniform(key_stiffness, (GRID_X, GRID_Y, 1, 1), jnp.float32, -0.69, 0.69))
    symmetric = (jitter + jnp.swapaxes(jitter, 2, 3)) * (spread * 0.70710678)
    identity = jnp.eye(order_size, dtype=jnp.float32)
    return (stiffness * (symmetric + identity * diagonal[..., None])).astype(jnp.bfloat16)


def shard_levels(own_key, dims, cuts, least, largest):
    level = 1.0
    for position, blocks in cuts:
        draws = jax.random.uniform(jax.random.fold_in(jax.random.fold_in(own_key, 6), position), (blocks,), jnp.float32, least / len(cuts), largest / len(cuts))
        level = level * jnp.repeat(jnp.exp(draws), dims[position] // blocks).reshape((-1,) + (1,) * (len(dims) - 1 - position))
    return level


def centred(stream_key, dims, scale, most, shards=(), held_as=jnp.bfloat16):
    factor_of = shard_levels(stream_key, dims, shards, -0.22, 0.18) if shards else 1.0
    array = jax.random.normal(stream_key, dims, jnp.float32) * scale * factor_of
    return jnp.minimum(jnp.maximum(array, -most), most).astype(held_as)


def setup_inputs(seed: int = 0) -> dict:
    streams_of = jax.random.split(jax.random.key(seed), 7)
    load_field = centred(streams_of[0], (GRID_X, GRID_Y, 2 * FACE, CASES), 1.0, 6.0, ((0, 64), (1, 8)), jnp.float32)
    schur_blocks = draw_schur_blocks(jax.random.fold_in(streams_of[6], 71), 0)
    local_inverse = draw_local_inverse(jax.random.fold_in(streams_of[6], 71), 0)
    face_order = jax.vmap(lambda own: jax.random.permutation(own, FACE))(jax.random.split(streams_of[3], GRID_X * GRID_Y * 2)).reshape((GRID_X, GRID_Y, 2, FACE)).astype(jnp.int32)
    coarse_weights = jnp.clip(jax.random.uniform(streams_of[4], (2 * FACE,), jnp.float32, 0.03, 0.12), 0.03, 0.12)
    coarse_decay = jnp.clip(jnp.exp(math.log(0.0390625) - 2.3025851 * jax.random.uniform(streams_of[5], (GRID_X, GRID_Y), jnp.float32) ** shard_levels(streams_of[5], (GRID_X, GRID_Y), ((0, 64), (1, 8)), -0.2, 0.2)), 0.00390625, 0.0390625)
    return {"load_field": load_field, "schur_blocks": schur_blocks, "local_inverse": local_inverse, "face_order": face_order, "coarse_weights": coarse_weights, "coarse_decay": coarse_decay}


def edge_open(grid_x, grid_y, face_count):
    first_open = (jnp.arange(grid_x, dtype=jnp.int32) < grid_x - 1).astype(jnp.float32)
    second_open = (jnp.arange(grid_y, dtype=jnp.int32) < grid_y - 1).astype(jnp.float32)
    east_open = jnp.broadcast_to(first_open[:, None, None, None], (grid_x, grid_y, face_count, 1))
    north_open = jnp.broadcast_to(second_open[None, :, None, None], (grid_x, grid_y, face_count, 1))
    return jnp.concatenate([east_open, north_open], axis=2)


def assemble(values, blocks, hot_high):
    face_count = hot_high.shape[-1]
    east_face = values[:, :, :face_count]
    north_face = values[:, :, face_count:]
    west_raw = jnp.concatenate([jnp.zeros_like(east_face[:1]), east_face[:-1]], axis=0)
    south_raw = jnp.concatenate([jnp.zeros_like(north_face[:, :1]), north_face[:, :-1]], axis=1)
    west_face = jnp.einsum("xyji,xyir->xyjr", hot_high[:, :, 0], west_raw.astype(jnp.float32), precision=lax.Precision.HIGHEST).astype(jnp.bfloat16)
    south_face = jnp.einsum("xyji,xyir->xyjr", hot_high[:, :, 1], south_raw.astype(jnp.float32), precision=lax.Precision.HIGHEST).astype(jnp.bfloat16)
    local_part = jnp.concatenate([east_face, north_face, west_face, south_face], axis=2).astype(jnp.float32)
    image_part = jnp.einsum("xyij,xyjr->xyir", blocks, local_part, precision=lax.Precision.HIGHEST)
    back_west = jnp.einsum("xyji,xyjr->xyir", hot_high[:, :, 0], image_part[:, :, 2 * face_count:3 * face_count], precision=lax.Precision.HIGHEST)
    back_south = jnp.einsum("xyji,xyjr->xyir", hot_high[:, :, 1], image_part[:, :, 3 * face_count:], precision=lax.Precision.HIGHEST)
    east_total = image_part[:, :, :face_count] + jnp.concatenate([back_west[1:], jnp.zeros_like(back_west[:1])], axis=0)
    north_total = image_part[:, :, face_count:2 * face_count] + jnp.concatenate([back_south[:, 1:], jnp.zeros_like(back_south[:, :1])], axis=1)
    return jnp.concatenate([east_total, north_total], axis=2)


def coarse_values(residual_field, weights, keep_rate):
    demand = jnp.einsum("k,xykr->xyr", weights, residual_field, precision=lax.Precision.HIGHEST)
    nothing = jnp.zeros(demand.shape[1:], jnp.float32)

    def forward(carried, element):
        carried = element[0][:, None] * carried + element[1]
        return carried, carried

    def backward(carried, element):
        summed = carried + element[1]
        return element[0][:, None] * summed, summed

    climbed = lax.scan(forward, nothing, (keep_rate, demand))[1]
    return lax.scan(backward, nothing, (keep_rate, climbed), reverse=True)[1]


def precondition(residual_field, inverse_blocks, hot_high, weights, keep_rate, opened):
    halved = (0.5 * residual_field).astype(jnp.bfloat16)
    assembled = assemble(halved, inverse_blocks, hot_high)
    settled = coarse_values(residual_field, weights, keep_rate)
    return opened * (0.5 * assembled + weights[None, None, :, None] * settled[:, :, None, :])


def reference(load_field, schur_blocks, local_inverse, face_order, coarse_weights, coarse_decay):
    face_count = face_order.shape[-1]
    opened = edge_open(load_field.shape[0], load_field.shape[1], face_count)
    hot_high = (face_order[..., :, None] == jnp.arange(face_count, dtype=jnp.int32)).astype(jnp.float32)
    schur_wide = schur_blocks.astype(jnp.float32)
    inverse_wide = local_inverse.astype(jnp.float32)
    keep_rate = jnp.exp(-coarse_decay)
    residual_field = opened * load_field
    solution_field = jnp.zeros_like(load_field)
    search = precondition(residual_field, inverse_wide, hot_high, coarse_weights, keep_rate, opened)
    inner_now = jnp.sum(residual_field * search, axis=(0, 1, 2))
    for number in range(ITERS):
        rounded = search.astype(jnp.bfloat16)
        product = opened * assemble(rounded, schur_wide, hot_high)
        curvature = jnp.sum(rounded.astype(jnp.float32) * product, axis=(0, 1, 2))
        step_size = inner_now / curvature
        solution_field = solution_field + step_size * search
        residual_field = residual_field - step_size * product
        if number + 1 < ITERS:
            smoothed = precondition(residual_field, inverse_wide, hot_high, coarse_weights, keep_rate, opened)
            inner_next = jnp.sum(residual_field * smoothed, axis=(0, 1, 2))
            search = smoothed + (inner_next / inner_now) * search
            inner_now = inner_next
    return solution_field
```

```python
import functools

import jax
import jax.numpy as jnp
from jax import lax
from jax.experimental import pallas as pl
from jax.experimental.pallas import tpu as pltpu
from jax.sharding import PartitionSpec as P

MESH = pl.DeviceIdType.MESH
F32 = jnp.float32
BF16 = jnp.bfloat16
SX, SY, FACE, CASES = 2, 4, 64, 256
LANES = 128


def kernel(
    ny, nz, ng,
    load_hbm, schur_hbm, inverse_hbm, order_hbm, weight_hbm, decay_hbm,
    s_out, t_out, coef_out,
    load, blocks_s, blocks_p, order, weight, decay,
    wcol, edge_w, north_w, acc_e, acc_n, send_e, send_n, recv_e, recv_n, q_field,
    dk, zbuf, climb_l, trans, fg, ybuf, line_in, settled_grp, settled, ghost_col,
    mom, abuf, reduced,
    in_sem, send_sem, recv_sem,
):
    gx, gy = lax.axis_index("gx"), lax.axis_index("gy")
    nx = ny * nz
    y, z = gx // nz, gx % nz
    z_peers = [(y * nz + (z + j) % nz, gy) for j in range(1, nz)]
    y_peers = [(((y + j) % ny) * nz + z, gy) for j in range(1, ny)]
    g_peers = [(gx, (gy + j) % ng) for j in range(1, ng)]
    east, west = ((gx + 1) % nx, gy), ((gx + nx - 1) % nx, gy)
    north, south = (gx, (gy + 1) % ng), (gx, (gy + ng - 1) % ng)

    barrier = pltpu.get_barrier_semaphore()
    greeted = z_peers + y_peers + g_peers + [east, west]
    for peer in greeted:
        pl.semaphore_signal(barrier, inc=1, device_id=peer, device_id_type=MESH)

    def fetch(k, src, dst):
        copy = pltpu.make_async_copy(src, dst, in_sem.at[k])
        copy.start()
        return copy

    load_in = fetch(0, load_hbm, load)
    small_in = [fetch(1, order_hbm, order), fetch(2, weight_hbm, weight), fetch(3, decay_hbm, decay)]
    inverse_in = fetch(4, inverse_hbm, blocks_p)
    schur_in = fetch(5, schur_hbm, blocks_s)

    sent = []

    def send(src, dst, peer):
        k = len(sent)
        copy = pltpu.make_async_remote_copy(
            src_ref=src, dst_ref=dst, send_sem=send_sem.at[k], recv_sem=recv_sem.at[k],
            device_id=peer, device_id_type=MESH,
        )
        copy.start()
        sent.append(copy)
        return copy

    def arrived(copies):
        for copy in copies:
            copy.wait_recv()

    east_open = (gx < nx - 1).astype(F32)
    west_open = (gx > 0).astype(F32)
    north_open = (gy < ng - 1).astype(F32)
    south_open = (gy > 0).astype(F32)

    load_in.wait()
    for b in range(SY):
        face = load[1, b, :FACE] * east_open
        load[1, b, :FACE] = face
        edge_w[0, 2, b] = face.astype(BF16)
    for a in range(SX):
        face = load[a, SY - 1, FACE:] * north_open
        load[a, SY - 1, FACE:] = face
        north_w[0, a, SY] = face.astype(BF16)
    pl.semaphore_wait(barrier, len(greeted))
    halo = [
        send(edge_w.at[0, 2], edge_w.at[0, 0], east),
        send(north_w.at[0, :, SY], north_w.at[0, :, 0], north),
    ]

    for copy in small_in:
        copy.wait()
    wcol[...] = jnp.transpose(jnp.broadcast_to(weight[...], (LANES, 2 * FACE)))

    def demand_tiles(field):
        for a in range(SX):
            for b in range(SY):
                for h in range(2):
                    lanes = slice(h * LANES, (h + 1) * LANES)
                    value = field[a, b, :, lanes] * wcol[...]
                    dk[a, 2 * b + h : 2 * b + h + 1] = jnp.sum(value, axis=0, keepdims=True)

    demand_tiles(load)
    keep = jnp.exp(-decay[...])
    for a in range(SX):
        for b in range(SY):
            dk[SX + a, 2 * b : 2 * b + 2] = jnp.broadcast_to(keep[a : a + 1, b : b + 1], (2, LANES))
    zbuf[0, z] = dk[...]
    gather_z = [send(dk, zbuf.at[0, z], peer) for peer in z_peers]

    for b in range(SY):
        edge_w[0, 1, b] = load[0, b, :FACE].astype(BF16)
    for a in range(SX):
        for b in range(SY - 1):
            north_w[0, a, b + 1] = load[a, b, FACE:].astype(BF16)

    def fold_order(blocks):
        row = lax.broadcasted_iota(jnp.int32, (2 * FACE, 2 * FACE), 0)
        for a in range(SX):
            for b in range(SY):
                own = order[a, b]
                place = jnp.concatenate([own[0:1], own[1:2] + FACE], axis=1)
                hot_t = (row == jnp.broadcast_to(place, (2 * FACE, 2 * FACE))).astype(F32).astype(BF16)
                columns = lax.dot_general(
                    blocks[a, b, :, 2 * FACE :], hot_t, (((1,), (1,)), ((), ())), preferred_element_type=F32
                )
                blocks[a, b, :, 2 * FACE :] = columns.astype(BF16)
                rows = jnp.dot(hot_t, blocks[a, b, 2 * FACE :, :], preferred_element_type=F32)
                blocks[a, b, 2 * FACE :, :] = rows.astype(BF16)

    inverse_in.wait()
    fold_order(blocks_p)

    def group_solve(turn, first):
        group = SX * nz
        climb = jnp.zeros((8, LANES), F32)
        for r in range(group):
            k = zbuf[0, r // SX, SX + r % SX]
            climb = k * climb + zbuf[turn, r // SX, r % SX]
            climb_l[r] = climb
        back = jnp.zeros((8, LANES), F32)
        for r in range(group - 1, -1, -1):
            back = zbuf[0, r // SX, SX + r % SX] * (back + climb_l[r])
        fg[turn, 0] = climb
        fg[turn, 1] = back
        if first:
            product = jnp.ones((8, LANES), F32)
            squares = jnp.zeros((8, LANES), F32)
            for r in range(group):
                product = product * zbuf[0, r // SX, SX + r % SX]
                trans[r] = product
                squares = squares + product * product
            fg[turn, 2] = product
            fg[turn, 3] = squares
        ybuf[turn, y] = fg[turn]
        if first:
            return [send(fg.at[turn], ybuf.at[turn, y], peer) for peer in y_peers]
        return [send(fg.at[turn, 0:2], ybuf.at[turn, y, 0:2], peer) for peer in y_peers]

    def line_finish(turn):
        group = SX * nz
        climb_in = jnp.zeros((8, LANES), F32)
        for j in range(ny):
            line_in[0, j] = climb_in
            climb_in = ybuf[0, j, 2] * climb_in + ybuf[turn, j, 0]
        back = jnp.zeros((8, LANES), F32)
        for j in range(ny - 1, -1, -1):
            line_in[1, j] = back
            back = ybuf[0, j, 2] * back + ybuf[turn, j, 1] + ybuf[0, j, 3] * line_in[0, j]
            line_in[2, j] = back
        climb_in = line_in[0, y]
        back = line_in[1, y]
        for r in range(group - 1, -1, -1):
            total = climb_l[r] + trans[r] * climb_in + back
            settled_grp[r + 1] = total
            back = zbuf[0, r // SX, SX + r % SX] * total
        settled_grp[0] = climb_in + line_in[2, y]
        for r in range(SX + 1):
            settled[turn, r] = settled_grp[SX * z + r]
        return [send(settled.at[turn, 1:3], ghost_col.at[turn], north)]

    def multiply(blocks, now, turn):
        total = jnp.zeros((8, CASES), F32)
        copies = []
        for a in (1, 0):
            for b in range(SY):
                field = jnp.concatenate(
                    [edge_w[now, a + 1, b], north_w[now, a, b + 1], edge_w[now, a, b], north_w[now, a, b]], axis=0
                )
                image = jnp.dot(blocks[a, b], field, preferred_element_type=F32)
                total = total + jnp.sum(
                    (image * field.astype(F32)).reshape(2 * FACE * 2 // 8, 8, CASES), axis=0
                )
                img_e, img_n = image[:FACE], image[FACE : 2 * FACE]
                img_w, img_s = image[2 * FACE : 3 * FACE], image[3 * FACE :]
                if a == 1:
                    acc_e[2, b] = img_e
                    send_e[turn, 0, b] = img_e.astype(BF16)
                    acc_e[1, b] = img_w
                else:
                    acc_e[1, b] = acc_e[1, b] + img_e
                    acc_e[0, b] = img_w
                    send_e[turn, 1, b] = img_w.astype(BF16)
                acc_n[a, b + 1] = img_n
                if b == 0:
                    acc_n[a, 0] = img_s
                    send_n[turn, 1, a] = img_s.astype(BF16)
                else:
                    acc_n[a, b] = acc_n[a, b] + img_s
                if b == SY - 1:
                    send_n[turn, 0, a] = img_n.astype(BF16)
            if turn < 3:
                if a == 1:
                    copies.append(send(send_e.at[turn, 0], recv_e.at[turn, 0], east))
                else:
                    copies.append(send(send_e.at[turn, 1], recv_e.at[turn, 1], west))
        if turn < 3:
            copies.append(send(send_n.at[turn, 0], recv_n.at[turn, 0], north))
            copies.append(send(send_n.at[turn, 1], recv_n.at[turn, 1], south))
        return total, copies

    def edge_sum(turn, r, b):
        if r == 0:
            return (acc_e[0, b] + recv_e[turn, 0, b].astype(F32)) * west_open
        if r == SX:
            return (acc_e[2, b] + recv_e[turn, 1, b].astype(F32)) * east_open
        return acc_e[r, b]

    def north_sum(turn, a, c):
        if c == 0:
            return (acc_n[a, 0] + recv_n[turn, 0, a].astype(F32)) * south_open
        if c == SY:
            return (acc_n[a, SY] + recv_n[turn, 1, a].astype(F32)) * north_open
        return acc_n[a, c]

    def smooth(turn, coarse, now, out):
        def coarse_part(rows, tile):
            return jnp.concatenate(
                [wcol[rows] * tile[0:1], wcol[rows] * tile[1:2]], axis=1
            )

        for r in range(SX + 1):
            for b in range(SY):
                value = coarse_part(slice(0, FACE), settled[coarse, r, 2 * b : 2 * b + 2])
                if r == 0:
                    value = value * west_open
                if r == SX:
                    value = value * east_open
                value = value + 0.25 * edge_sum(turn, r, b)
                edge_w[now, r, b] = value.astype(BF16)
                if r > 0:
                    out[r - 1, b, :FACE] = value
        for a in range(SX):
            for c in range(SY + 1):
                if c == 0:
                    value = coarse_part(slice(FACE, 2 * FACE), ghost_col[coarse, a, 6:8]) * south_open
                else:
                    value = coarse_part(slice(FACE, 2 * FACE), settled[coarse, a + 1, 2 * c - 2 : 2 * c])
                if c == SY:
                    value = value * north_open
                value = value + 0.25 * north_sum(turn, a, c)
                north_w[now, a, c] = value.astype(BF16)
                if c > 0:
                    out[a, c - 1, FACE:] = value

    def dot(left, right):
        total = jnp.zeros((8, CASES), F32)
        for a in range(SX):
            for b in range(SY):
                total = total + jnp.sum((left[a, b] * right[a, b]).reshape(2 * FACE // 8, 8, CASES), axis=0)
        return total

    arrived(gather_z)
    gather_y = group_solve(0, True)
    arrived(halo)
    _, halo = multiply(blocks_p, 0, 0)
    schur_in.wait()
    fold_order(blocks_s)
    arrived(gather_y)
    column = line_finish(0)
    arrived(halo)
    arrived(column)
    smooth(0, 0, 1, s_out)

    moment1, halo = multiply(blocks_s, 1, 1)
    moment0 = dot(load, s_out)
    arrived(halo)
    for r in range(SX + 1):
        for b in range(SY):
            value = edge_sum(1, r, b)
            edge_w[2, r, b] = value.astype(BF16)
            if r > 0:
                q_field[r - 1, b, :FACE] = value
    for a in range(SX):
        for c in range(SY + 1):
            value = north_sum(1, a, c)
            north_w[2, a, c] = value.astype(BF16)
            if c > 0:
                q_field[a, c - 1, FACE:] = value
    for copy in gather_z:
        copy.wait_send()
    demand_tiles(q_field)
    zbuf[1, z] = dk[...]
    gather_z2 = [send(dk.at[0:2], zbuf.at[1, z, 0:2], peer) for peer in z_peers]
    _, halo = multiply(blocks_p, 2, 2)
    arrived(gather_z2)
    gather_y2 = group_solve(1, False)
    arrived(gather_y2)
    column = line_finish(1)
    arrived(halo)
    arrived(column)
    smooth(2, 1, 3, t_out)
    moment3, _ = multiply(blocks_s, 3, 3)
    moment2 = dot(q_field, t_out)

    for m, value in enumerate((moment0, moment1, moment2, moment3)):
        whole = jnp.sum(value, axis=0, keepdims=True)
        for h in range(2):
            mom[0, 2 * m + h : 2 * m + h + 1] = whole[:, h * LANES : (h + 1) * LANES]

    for stage, (peers, count, me) in enumerate(((g_peers, ng, gy), (z_peers, nz, z), (y_peers, ny, y))):
        abuf[stage, me] = mom[stage]
        copies = [send(mom.at[stage], abuf.at[stage, me], peer) for peer in peers]
        arrived(copies)
        value = abuf[stage, 0]
        for j in range(1, count):
            value = value + abuf[stage, j]
        if stage < 2:
            mom[stage + 1] = value
        else:
            reduced[...] = value

    m0, m1, m2, m3 = (reduced[2 * m : 2 * m + 2] for m in range(4))
    step0 = m0 / m1
    inner1 = step0 * step0 * m2 - m0
    beta = inner1 / m0
    mixed = m1 - step0 * m2
    curvature1 = mixed - step0 * m2 + step0 * step0 * m3 + 2.0 * beta * mixed + beta * beta * m1
    step1 = inner1 / curvature1
    coef_out[0:2] = step0 + step1 * (1.0 + beta)
    coef_out[2:4] = -step0 * step1

    waited = set(id(copy) for copy in gather_z)
    for copy in sent:
        if id(copy) not in waited:
            copy.wait_send()


def local(mesh_sizes, load_field, schur_blocks, local_inverse, face_order, coarse_weights, coarse_decay):
    ny, nz, ng = mesh_sizes
    big = max(ny, nz, ng)
    n_sends = 2 + 3 * 4 + 2 * (nz - 1 + ny - 1) + 2 + (ng - 1 + nz - 1 + ny - 1)
    field = (SX, SY, 2 * FACE, CASES)
    vmem = pl.BlockSpec(memory_space=pltpu.VMEM)
    s_field, t_field, coef = pl.pallas_call(
        functools.partial(kernel, ny, nz, ng),
        out_shape=[
            jax.ShapeDtypeStruct(field, F32),
            jax.ShapeDtypeStruct(field, F32),
            jax.ShapeDtypeStruct((4, LANES), F32),
        ],
        in_specs=[pl.BlockSpec(memory_space=pl.ANY)] * 6,
        out_specs=[vmem] * 3,
        scratch_shapes=[
            pltpu.VMEM(field, F32),
            pltpu.VMEM((SX, SY, 4 * FACE, 4 * FACE), BF16),
            pltpu.VMEM((SX, SY, 4 * FACE, 4 * FACE), BF16),
            pltpu.VMEM((SX, SY, 2, FACE), jnp.int32),
            pltpu.VMEM((1, 2 * FACE), F32),
            pltpu.VMEM((SX, SY), F32),
            pltpu.VMEM((2 * FACE, LANES), F32),
            pltpu.VMEM((4, SX + 1, SY, FACE, CASES), BF16),
            pltpu.VMEM((4, SX, SY + 1, FACE, CASES), BF16),
            pltpu.VMEM((SX + 1, SY, FACE, CASES), F32),
            pltpu.VMEM((SX, SY + 1, FACE, CASES), F32),
            pltpu.VMEM((4, 2, SY, FACE, CASES), BF16),
            pltpu.VMEM((4, 2, SX, FACE, CASES), BF16),
            pltpu.VMEM((3, 2, SY, FACE, CASES), BF16),
            pltpu.VMEM((3, 2, SX, FACE, CASES), BF16),
            pltpu.VMEM(field, F32),
            pltpu.VMEM((2 * SX, 8, LANES), F32),
            pltpu.VMEM((2, nz, 2 * SX, 8, LANES), F32),
            pltpu.VMEM((SX * nz, 8, LANES), F32),
            pltpu.VMEM((SX * nz, 8, LANES), F32),
            pltpu.VMEM((2, 4, 8, LANES), F32),
            pltpu.VMEM((2, ny, 4, 8, LANES), F32),
            pltpu.VMEM((3, ny, 8, LANES), F32),
            pltpu.VMEM((SX * nz + 1, 8, LANES), F32),
            pltpu.VMEM((2, SX + 1, 8, LANES), F32),
            pltpu.VMEM((2, SX, 8, LANES), F32),
            pltpu.VMEM((3, 8, LANES), F32),
            pltpu.VMEM((3, big, 8, LANES), F32),
            pltpu.VMEM((8, LANES), F32),
            pltpu.SemaphoreType.DMA((6,)),
            pltpu.SemaphoreType.DMA((n_sends,)),
            pltpu.SemaphoreType.DMA((n_sends,)),
        ],
        compiler_params=pltpu.CompilerParams(
            collective_id=0, has_side_effects=True, vmem_limit_bytes=40 << 20
        ),
        cost_estimate=pl.CostEstimate(flops=1_100_000_000, bytes_accessed=6 << 20, transcendentals=8),
    )(load_field, schur_blocks, local_inverse, face_order, coarse_weights.reshape(1, -1), coarse_decay)
    first, second = coef[0:2].reshape(CASES), coef[2:4].reshape(CASES)
    return first * s_field + second * t_field


def solution(mesh):
    nx, ng = mesh.shape["gx"], mesh.shape["gy"]
    nz = 8 if nx % 8 == 0 else 2
    in_specs = (
        P("gx", "gy", None, None),
        P("gx", "gy", None, None),
        P("gx", "gy", None, None),
        P("gx", "gy", None, None),
        P(),
        P("gx", "gy"),
    )
    return jax.shard_map(
        functools.partial(local, (nx // nz, nz, ng)),
        mesh=mesh, in_specs=in_specs, out_specs=P("gx", "gy", None, None), check_vma=False,
    )
```

```python
import functools

import jax
import jax.numpy as jnp
from jax import lax
from jax.experimental import pallas as pl
from jax.experimental.pallas import tpu as pltpu
from jax.sharding import PartitionSpec as P

MESH = pl.DeviceIdType.MESH
F32 = jnp.float32
BF16 = jnp.bfloat16
SX, SY, FACE, CASES = 2, 4, 64, 256
LANES = 128
TILE = 8
ORDER = (3, 2, 1, 0)
PLACE0, PLACE1 = 0, 0
CUT = 1


def kernel(
    ny, nz, ng,
    load_hbm, schur_hbm, inverse_hbm, order_hbm, weight_hbm, decay_hbm,
    s_hbm, t_hbm, coef_out,
    s_out, t_out, load, blocks_s, blocks_p, order, weight, decay,
    wcol, edge_w, north_w, acc_e, acc_n, send_e, send_n, recv_e, recv_n,
    ksrc, kz, kw, ykw, zsrc, za, zs, south_part, d_all, k_all, climb_l, trans, fg, ybuf, line_in,
    settled_grp, settled, ghost_col,
    mom, mid, sum_a, sum_b, mom3, mid3, sum3_a, sum3_b,
    in_sem, send_sem, recv_sem,
):
    gx, gy = lax.axis_index("gx"), lax.axis_index("gy")
    nx, nc, group = ny * nz, ng // 2, SX * nz
    y, z, x, core = gx // nz, gx % nz, gy // 2, gy % 2
    east, west = ((gx + 1) % nx, gy), ((gx + nx - 1) % nx, gy)
    north, south = (gx, (gy + 1) % ng), (gx, (gy + ng - 1) % ng)

    def ring(j):
        return y * nz + (z + j) % nz

    z_peers = [(ring(j), gy) for j in range(1, nz)]
    y_peers = [(((y + j) % ny) * nz + z, gy) for j in range(1, ny)]
    zn_peers = [(ring(j), (gy + 1) % ng) for j in range(nz)]
    zs_peers = [(ring(j), (gy + ng - 1) % ng) for j in range(nz)]
    a_peers = z_peers + [(ring(j), 2 * x + (1 - core)) for j in range(nz)]
    b_peers = [
        (((y + j) % ny) * nz + z, 2 * ((x + i) % nc) + core) for j in range(ny) for i in range(nc) if i + j
    ]

    barrier = pltpu.get_barrier_semaphore()
    greeted = [east, west, north, south] + zn_peers + zs_peers + a_peers + b_peers
    for peer in greeted:
        pl.semaphore_signal(barrier, inc=1, device_id=peer, device_id_type=MESH)

    fetched = []

    def fetch(src, dst):
        copy = pltpu.make_async_copy(src, dst, in_sem.at[len(fetched)])
        copy.start()
        fetched.append(copy)
        return copy

    decay_in = fetch(decay_hbm, decay)
    load_cut = [
        fetch(load_hbm.at[1, :, :FACE], load.at[1, :, :FACE]),
        fetch(load_hbm.at[:, SY - 1, FACE:], load.at[:, SY - 1, FACE:]),
    ]
    small_in = [fetch(order_hbm, order), fetch(weight_hbm, weight)]
    load_rest = [
        fetch(load_hbm.at[0, :, :FACE], load.at[0, :, :FACE]),
        fetch(load_hbm.at[:, : SY - 1, FACE:], load.at[:, : SY - 1, FACE:]),
    ]
    inverse_in = fetch(inverse_hbm, blocks_p)
    schur_in = fetch(schur_hbm, blocks_s)

    sent = []

    def send(src, dst, peer):
        k = len(sent)
        copy = pltpu.make_async_remote_copy(
            src_ref=src, dst_ref=dst, send_sem=send_sem.at[k], recv_sem=recv_sem.at[k],
            device_id=peer, device_id_type=MESH,
        )
        copy.start()
        sent.append(copy)
        return copy

    def arrived(copies):
        for copy in copies:
            copy.wait_recv()

    east_open = (gx < nx - 1).astype(F32)
    west_open = (gx > 0).astype(F32)
    north_open = (gy < ng - 1).astype(F32)
    south_open = (gy > 0).astype(F32)

    decay_in.wait()
    ksrc[...] = jnp.zeros((SX, LANES), F32)
    ksrc[:, 0:SY] = jnp.exp(-decay[...])
    kz[z] = ksrc[...]
    for copy in load_cut:
        copy.wait()
    for b in range(SY):
        face = load[1, b, :FACE] * east_open
        load[1, b, :FACE] = face
        edge_w[0, 2, b] = face.astype(BF16)
    for a in range(SX):
        face = load[a, SY - 1, FACE:] * north_open
        load[a, SY - 1, FACE:] = face
        north_w[0, a, SY] = face.astype(BF16)
    pl.semaphore_wait(barrier, len(greeted))
    gather_k = [send(ksrc, kz.at[z], peer) for peer in z_peers]
    halo_n = [send(north_w.at[0, :, SY], north_w.at[0, :, 0], north)]
    halo_e = {
        b + CUT - 1: [send(edge_w.at[0, 2, b : b + CUT], edge_w.at[0, 0, b : b + CUT], east)]
        for b in range(SY - CUT, -1, -CUT)
    }

    for copy in small_in + load_rest:
        copy.wait()
    wcol[...] = jnp.transpose(jnp.broadcast_to(weight[...], (LANES, 2 * FACE)))
    w_east, w_north = wcol[:FACE], wcol[FACE:]

    def weigh(face, weights):
        value = [jnp.sum(face[:, h * LANES : (h + 1) * LANES] * weights, axis=0, keepdims=True) for h in range(2)]
        return jnp.concatenate(value, axis=0)

    def gather_ring(turn, rows):
        za[turn, z, 0:rows] = zsrc[turn, 0:rows]
        copies = []
        if turn:
            copies += [send(south_part, zs.at[z], peer) for peer in zs_peers]
        copies += [send(zsrc.at[turn, 0:rows], za.at[turn, z, 0:rows], peer) for peer in z_peers]
        return copies

    for a in range(SX):
        for b in range(SY):
            rows = slice(2 * b, 2 * b + 2)
            zsrc[0, a, rows] = weigh(load[a, b, :FACE], w_east) + weigh(load[a, b, FACE:], w_north)
    gather_z = gather_ring(0, SX)

    for b in range(SY):
        edge_w[0, 1, b] = load[0, b, :FACE].astype(BF16)
    for a in range(SX):
        for b in range(SY - 1):
            north_w[0, a, b + 1] = load[a, b, FACE:].astype(BF16)

    def fold_order(blocks):
        row = lax.broadcasted_iota(jnp.int32, (2 * FACE, 2 * FACE), 0)
        for a in range(SX):
            for b in range(SY):
                own = order[a, b]
                place = jnp.concatenate([own[0:1], own[1:2] + FACE], axis=1)
                hot_t = (row == jnp.broadcast_to(place, (2 * FACE, 2 * FACE))).astype(F32).astype(BF16)
                columns = lax.dot_general(
                    blocks[a, b, :, 2 * FACE :], hot_t, (((1,), (1,)), ((), ())), preferred_element_type=F32
                )
                blocks[a, b, :, 2 * FACE :] = columns.astype(BF16)
                rows = jnp.dot(hot_t, blocks[a, b, 2 * FACE :, :], preferred_element_type=F32)
                blocks[a, b, 2 * FACE :, :] = rows.astype(BF16)

    inverse_in.wait()
    fold_order(blocks_p)

    def group_keep():
        for r in range(group):
            for b in range(SY):
                rate = kz[r // SX, r % SX : r % SX + 1, b : b + 1]
                k_all[r, 2 * b : 2 * b + 2] = jnp.broadcast_to(rate, (2, LANES))
        product = jnp.ones((TILE, LANES), F32)
        squares = jnp.zeros((TILE, LANES), F32)
        for r in range(group):
            product = product * k_all[r]
            trans[r] = product
            squares = squares + product * product
        kw[0] = product
        kw[1] = squares
        ykw[y] = kw[...]
        return [send(kw, ykw.at[y], peer) for peer in y_peers]

    def group_solve(turn):
        for r in range(group):
            s, a = r // SX, r % SX
            if turn == 0:
                d_all[turn, r] = za[0, s, a]
            else:
                own = za[1, s, a + 1]
                if a == SX - 1 and s + 1 < nz:
                    own = own + za[1, s + 1, 0]
                d_all[turn, r] = own
                d_all[turn, r, 6:8] = d_all[turn, r, 6:8] + zs[s, a]
        climb = jnp.zeros((TILE, LANES), F32)
        for r in range(group):
            climb = k_all[r] * climb + d_all[turn, r]
            climb_l[turn, r] = climb
        back = jnp.zeros((TILE, LANES), F32)
        for r in range(group - 1, -1, -1):
            back = k_all[r] * (back + climb_l[turn, r])
        fg[turn, 0] = climb
        fg[turn, 1] = back
        if turn:
            fg[turn, 2] = za[1, 0, 0]
        count = 2 + turn
        ybuf[turn, y, 0:count] = fg[turn, 0:count]
        return [send(fg.at[turn, 0:count], ybuf.at[turn, y, 0:count], peer) for peer in y_peers]

    pending = {}

    def line_finish(turn):
        climb_in = jnp.zeros((TILE, LANES), F32)
        for j in range(ny):
            line_in[0, j] = climb_in
            climb_in = ykw[j, 0] * climb_in + ybuf[turn, j, 0]
            if turn:
                climb_in = climb_in + ybuf[1, (j + 1) % ny, 2]
        back = jnp.zeros((TILE, LANES), F32)
        for j in range(ny - 1, -1, -1):
            line_in[1, j] = back
            if turn:
                back = back + ybuf[1, (j + 1) % ny, 2]
            back = ykw[j, 0] * back + ybuf[turn, j, 1] + ykw[j, 1] * line_in[0, j]
            line_in[2, j] = back
        climb_in = line_in[0, y]
        back = line_in[1, y]
        if turn:
            handed = ybuf[1, (y + 1) % ny, 2]
            back = back + handed
            d_all[turn, group - 1] = d_all[turn, group - 1] + handed
        for r in range(group - 1, -1, -1):
            total = climb_l[turn, r] + trans[r] * climb_in + back
            settled_grp[turn, r + 1] = total
            back = k_all[r] * total
        settled_grp[turn, 0] = climb_in + line_in[2, y]
        total = jnp.zeros((8, LANES), F32)
        for r in range(SX + 1):
            value = settled_grp[turn, SX * z + r]
            settled[turn, r] = value
            if r == SX:
                pending["column"] = [send(settled.at[turn, 1:3, 6:8], ghost_col.at[turn], north)]
            if r:
                total = total + value[0:8] * d_all[turn, SX * z + r - 1, 0:8]
        return total[0:2] + total[2:4] + total[4:6] + total[6:8]

    def edge_sum(turn, r, b):
        if r == 0:
            return (acc_e[turn % 2, 0, b] + recv_e[turn, 0, b].astype(F32)) * west_open
        if r == SX:
            return (acc_e[turn % 2, 2, b] + recv_e[turn, 1, b].astype(F32)) * east_open
        return acc_e[turn % 2, r, b]

    def north_sum(turn, a, c):
        if c == 0:
            return (acc_n[turn % 2, a, 0] + recv_n[turn, 0, a].astype(F32)) * south_open
        if c == SY:
            return (acc_n[turn % 2, a, SY] + recv_n[turn, 1, a].astype(F32)) * north_open
        return acc_n[turn % 2, a, c]

    def spread(weights, pair):
        return jnp.concatenate([weights * pair[0:1], weights * pair[1:2]], axis=1)

    def edge_face(turn, coarse, out, r, b):
        value = edge_sum(turn, r, b)
        if coarse is not None:
            part = spread(w_east, settled[coarse, r, 2 * b : 2 * b + 2])
            if r == 0:
                part = part * west_open
            if r == SX:
                part = part * east_open
            value = 0.25 * value + part
            if r > 0:
                out[r - 1, b, :FACE] = value
        edge_w[turn + 1, r, b] = value.astype(BF16)

    def north_face(turn, coarse, out, a, c):
        value = north_sum(turn, a, c)
        if coarse is not None:
            pair = settled[coarse, a + 1, 2 * c - 2 : 2 * c] if c else ghost_col[coarse, a]
            part = spread(w_north, pair)
            if c == 0:
                part = part * south_open
            if c == SY:
                part = part * north_open
            value = 0.25 * value + part
            if c > 0:
                out[a, c - 1, FACE:] = value
        north_w[turn + 1, a, c] = value.astype(BF16)

    def stage(turn, blocks, halo_e, halo_n, coarse=None, out=None, between=None):
        if turn > 0:
            for b in range(SY):
                edge_face(turn - 1, coarse, out, 1, b)
            for a in range(SX):
                for c in range(1, SY):
                    north_face(turn - 1, coarse, out, a, c)
        now = turn % 2
        total = jnp.zeros((8, CASES), F32)
        next_e, next_n = {}, []
        for place, b in enumerate(ORDER):
            if between is not None and place == between[0]:
                between[1]()
            if turn == 0:
                if b == 0:
                    arrived(halo_n)
            elif b == SY - 1:
                arrived(halo_n[1])
                for a in range(SX):
                    north_face(turn - 1, coarse, out, a, SY)
            elif b == 0:
                arrived(halo_n[0])
                if coarse is not None:
                    arrived(pending["column"])
                for a in range(SX):
                    north_face(turn - 1, coarse, out, a, 0)
            if b in halo_e:
                arrived(halo_e[b])
            if turn > 0:
                edge_face(turn - 1, coarse, out, 2, b)
                edge_face(turn - 1, coarse, out, 0, b)
            for a in (1, 0):
                field = jnp.concatenate(
                    [edge_w[turn, a + 1, b], north_w[turn, a, b + 1], edge_w[turn, a, b], north_w[turn, a, b]], axis=0
                )
                image = jnp.dot(blocks[a, b], field, preferred_element_type=F32)
                total = total + jnp.sum((image * field.astype(F32)).reshape(4 * FACE // 8, 8, CASES), axis=0)
                if turn == 3:
                    continue
                img_e, img_n = image[:FACE], image[FACE : 2 * FACE]
                img_w, img_s = image[2 * FACE : 3 * FACE], image[3 * FACE :]
                if a == 1:
                    acc_e[now, 2, b] = img_e
                    send_e[turn, 0, b] = img_e.astype(BF16)
                    acc_e[now, 1, b] = img_w
                else:
                    acc_e[now, 1, b] = acc_e[now, 1, b] + img_e
                    acc_e[now, 0, b] = img_w
                    send_e[turn, 1, b] = img_w.astype(BF16)
                if b == SY - 1:
                    acc_n[now, a, b + 1] = img_n
                else:
                    acc_n[now, a, b + 1] = acc_n[now, a, b + 1] + img_n
                acc_n[now, a, b] = img_s
                if b == 0:
                    send_n[turn, 1, a] = img_s.astype(BF16)
                if b == SY - 1:
                    send_n[turn, 0, a] = img_n.astype(BF16)
            if turn == 3:
                continue
            if b % CUT == 0:
                some = slice(b, b + CUT)
                next_e[b + CUT - 1] = [
                    send(send_e.at[turn, 0, some], recv_e.at[turn, 0, some], east),
                    send(send_e.at[turn, 1, some], recv_e.at[turn, 1, some], west),
                ]
            if b == SY - 1:
                to_north = send(send_n.at[turn, 0], recv_n.at[turn, 0], north)
            if b == 0:
                to_south = send(send_n.at[turn, 1], recv_n.at[turn, 1], south)
        if turn < 3:
            next_n = [[to_north], [to_south]]
        if between is not None and between[0] == SY:
            between[1]()
        return total, next_e, next_n

    def by_half(total):
        whole = jnp.sum(total, axis=0, keepdims=True)
        return jnp.concatenate([whole[:, :LANES], whole[:, LANES:]], axis=0)

    def all_sum(source, middle, buf_a, buf_b):
        def first():
            buf_a[2 * z + core] = source[...]
            return [send(source, buf_a.at[2 * z + core], peer) for peer in a_peers]

        def second(copies):
            arrived(copies)
            value = buf_a[0]
            for k in range(1, 2 * nz):
                value = value + buf_a[k]
            middle[...] = value
            buf_b[nc * y + x] = value
            return [send(middle, buf_b.at[nc * y + x], peer) for peer in b_peers]

        def third(copies):
            arrived(copies)
            value = buf_b[0]
            for k in range(1, ny * nc):
                value = value + buf_b[k]
            return value

        return first, second, third

    def solve_ring(turn, copies):
        def run():
            if turn == 0:
                arrived(gather_k)
                pending["keep"] = group_keep()
            arrived(copies)
            pending[turn] = group_solve(turn)

        return run

    total0, halo_e, halo_n = stage(0, blocks_p, halo_e, halo_n, between=(PLACE0, solve_ring(0, gather_z)))
    schur_in.wait()
    fold_order(blocks_s)
    arrived(pending["keep"])
    arrived(pending[0])
    coarse0 = line_finish(0)
    total1, halo_e, halo_n = stage(1, blocks_s, halo_e, halo_n, 0, s_out)

    s_done = fetch(s_out, s_hbm)
    for b in range(SY):
        rows = slice(2 * b, 2 * b + 2)
        zsrc[1, 0, rows] = weigh(acc_e[1, 0, b], w_east) * west_open
        for a in range(SX):
            part_e, part_n = weigh(acc_e[1, a + 1, b], w_east), weigh(acc_n[1, a, b + 1], w_north)
            if a == SX - 1:
                part_e = part_e * east_open
            if b == SY - 1:
                part_n = part_n * north_open
            zsrc[1, a + 1, rows] = part_e + part_n
    for a in range(SX):
        south_part[a] = weigh(acc_n[1, a, 0], w_north) * south_open
    gather_z = gather_ring(1, SX + 1)

    mom[0:2] = 0.25 * by_half(total0) + coarse0
    mom[2:4] = by_half(total1)
    mom[6:8] = jnp.zeros((2, LANES), F32)

    total2, halo_e, halo_n = stage(2, blocks_p, halo_e, halo_n, between=(PLACE1, solve_ring(1, gather_z)))
    arrived(pending[1])
    coarse1 = line_finish(1)
    mom[4:6] = 0.25 * by_half(total2) + coarse1
    early = all_sum(mom, mid, sum_a, sum_b)
    early_a = early[0]()

    total3, _, _ = stage(3, blocks_s, halo_e, halo_n, 1, t_out)
    mom3[...] = by_half(total3)
    t_done = fetch(t_out, t_hbm)
    late = all_sum(mom3, mid3, sum3_a, sum3_b)
    late_a = late[0]()
    early_b = early[1](early_a)
    late_b = late[1](late_a)
    reduced = early[2](early_b)
    m3 = late[2](late_b)
    m0, m1, m2 = reduced[0:2], reduced[2:4], reduced[4:6]
    step0 = m0 / m1
    inner1 = step0 * step0 * m2 - m0
    beta = inner1 / m0
    mixed = m1 - step0 * m2
    curvature1 = mixed - step0 * m2 + step0 * step0 * m3 + 2.0 * beta * mixed + beta * beta * m1
    step1 = inner1 / curvature1
    coef_out[0:2] = step0 + step1 * (1.0 + beta)
    coef_out[2:4] = -step0 * step1

    s_done.wait()
    t_done.wait()
    for copy in sent:
        copy.wait_send()


def local(mesh_sizes, load_field, schur_blocks, local_inverse, face_order, coarse_weights, coarse_decay):
    ny, nz, ng = mesh_sizes
    nc, group = ng // 2, SX * nz
    n_sends = 1 + 3 * 2 + 7 * (SY // CUT) + 3 * (nz - 1 + ny - 1) + nz + 2 + 2 * (2 * nz - 1 + ny * nc - 1)
    field = (SX, SY, 2 * FACE, CASES)
    vmem = pl.BlockSpec(memory_space=pltpu.VMEM)
    s_field, t_field, coef = pl.pallas_call(
        functools.partial(kernel, ny, nz, ng),
        out_shape=[
            jax.ShapeDtypeStruct(field, F32),
            jax.ShapeDtypeStruct(field, F32),
            jax.ShapeDtypeStruct((4, LANES), F32),
        ],
        in_specs=[pl.BlockSpec(memory_space=pltpu.HBM)] * 6,
        out_specs=[pl.BlockSpec(memory_space=pltpu.HBM)] * 2 + [vmem],
        scratch_shapes=[
            pltpu.VMEM(field, F32),
            pltpu.VMEM(field, F32),
            pltpu.VMEM(field, F32),
            pltpu.VMEM((SX, SY, 4 * FACE, 4 * FACE), BF16),
            pltpu.VMEM((SX, SY, 4 * FACE, 4 * FACE), BF16),
            pltpu.VMEM((SX, SY, 2, FACE), jnp.int32),
            pltpu.VMEM((1, 2 * FACE), F32),
            pltpu.VMEM((SX, SY), F32),
            pltpu.VMEM((2 * FACE, LANES), F32),
            pltpu.VMEM((4, SX + 1, SY, FACE, CASES), BF16),
            pltpu.VMEM((4, SX, SY + 1, FACE, CASES), BF16),
            pltpu.VMEM((2, SX + 1, SY, FACE, CASES), F32),
            pltpu.VMEM((2, SX, SY + 1, FACE, CASES), F32),
            pltpu.VMEM((3, 2, SY, FACE, CASES), BF16),
            pltpu.VMEM((3, 2, SX, FACE, CASES), BF16),
            pltpu.VMEM((3, 2, SY, FACE, CASES), BF16),
            pltpu.VMEM((3, 2, SX, FACE, CASES), BF16),
            pltpu.VMEM((SX, LANES), F32),
            pltpu.VMEM((nz, SX, LANES), F32),
            pltpu.VMEM((2, TILE, LANES), F32),
            pltpu.VMEM((ny, 2, TILE, LANES), F32),
            pltpu.VMEM((2, SX + 1, TILE, LANES), F32),
            pltpu.VMEM((2, nz, SX + 1, TILE, LANES), F32),
            pltpu.VMEM((nz, SX, 2, LANES), F32),
            pltpu.VMEM((SX, 2, LANES), F32),
            pltpu.VMEM((2, group, TILE, LANES), F32),
            pltpu.VMEM((group, TILE, LANES), F32),
            pltpu.VMEM((2, group, TILE, LANES), F32),
            pltpu.VMEM((group, TILE, LANES), F32),
            pltpu.VMEM((2, 3, TILE, LANES), F32),
            pltpu.VMEM((2, ny, 3, TILE, LANES), F32),
            pltpu.VMEM((3, ny, TILE, LANES), F32),
            pltpu.VMEM((2, group + 1, TILE, LANES), F32),
            pltpu.VMEM((2, SX + 1, TILE, LANES), F32),
            pltpu.VMEM((2, SX, 2, LANES), F32),
            pltpu.VMEM((8, LANES), F32),
            pltpu.VMEM((8, LANES), F32),
            pltpu.VMEM((2 * nz, 8, LANES), F32),
            pltpu.VMEM((ny * nc, 8, LANES), F32),
            pltpu.VMEM((2, LANES), F32),
            pltpu.VMEM((2, LANES), F32),
            pltpu.VMEM((2 * nz, 2, LANES), F32),
            pltpu.VMEM((ny * nc, 2, LANES), F32),
            pltpu.SemaphoreType.DMA((11,)),
            pltpu.SemaphoreType.DMA((n_sends,)),
            pltpu.SemaphoreType.DMA((n_sends,)),
        ],
        compiler_params=pltpu.CompilerParams(
            collective_id=0, has_side_effects=True, vmem_limit_bytes=60 << 20
        ),
        cost_estimate=pl.CostEstimate(flops=1_100_000_000, bytes_accessed=6 << 20, transcendentals=8),
    )(load_field, schur_blocks, local_inverse, face_order, coarse_weights.reshape(1, -1), coarse_decay)
    first, second = coef[0:2].reshape(CASES), coef[2:4].reshape(CASES)
    return first * s_field + second * t_field


def solution(mesh):
    nx, ng = mesh.shape["gx"], mesh.shape["gy"]
    nz = 8 if nx % 8 == 0 else 2
    in_specs = (
        P("gx", "gy", None, None),
        P("gx", "gy", None, None),
        P("gx", "gy", None, None),
        P("gx", "gy", None, None),
        P(),
        P("gx", "gy"),
    )
    return jax.shard_map(
        functools.partial(local, (nx // nz, nz, ng)),
        mesh=mesh, in_specs=in_specs, out_specs=P("gx", "gy", None, None), check_vma=False,
    )
```

```python
import functools

import jax
import jax.numpy as jnp
from jax import lax
from jax.experimental import pallas as pl
from jax.experimental.pallas import tpu as pltpu
from jax.sharding import PartitionSpec as P

MESH = pl.DeviceIdType.MESH
F32 = jnp.float32
BF16 = jnp.bfloat16
SX, SY, FACE, CASES = 2, 4, 64, 256
LANES = 128
TILE = 8
ORDER = (3, 2, 1, 0)
PLACE0, PLACE1 = 0, 0
CUT = 1


def kernel(
    ny, nz, ng,
    load_hbm, schur_hbm, inverse_hbm, order_hbm, weight_hbm, decay_hbm,
    x_hbm,
    s_out, t_out, load, blocks_s, blocks_p, order, weight, decay,
    wcol, edge_w, north_w, acc_e, acc_n, send_e, send_n, recv_e, recv_n,
    ksrc, kz, kw, ykw, zsrc, za, zs, south_part, d_all, k_all, climb_l, trans, fg, ybuf, line_in,
    settled_grp, settled, ghost_col,
    mom, mid, sum_a, sum_b, mom3, mid3, sum3_a, sum3_b,
    in_sem, send_sem, recv_sem,
):
    gx, gy = lax.axis_index("gx"), lax.axis_index("gy")
    nx, nc, group = ny * nz, ng // 2, SX * nz
    y, z, x, core = gx // nz, gx % nz, gy // 2, gy % 2
    east, west = ((gx + 1) % nx, gy), ((gx + nx - 1) % nx, gy)
    north, south = (gx, (gy + 1) % ng), (gx, (gy + ng - 1) % ng)

    def ring(j):
        return y * nz + (z + j) % nz

    z_peers = [(ring(j), gy) for j in range(1, nz)]
    y_peers = [(((y + j) % ny) * nz + z, gy) for j in range(1, ny)]
    zn_peers = [(ring(j), (gy + 1) % ng) for j in range(nz)]
    zs_peers = [(ring(j), (gy + ng - 1) % ng) for j in range(nz)]
    a_peers = z_peers + [(ring(j), 2 * x + (1 - core)) for j in range(nz)]
    b_peers = [
        (((y + j) % ny) * nz + z, 2 * ((x + i) % nc) + core) for j in range(ny) for i in range(nc) if i + j
    ]

    barrier = pltpu.get_barrier_semaphore()
    greeted = [east, west, north, south] + zn_peers + zs_peers + a_peers + b_peers
    for peer in greeted:
        pl.semaphore_signal(barrier, inc=1, device_id=peer, device_id_type=MESH)

    fetched = []

    def fetch(src, dst):
        copy = pltpu.make_async_copy(src, dst, in_sem.at[len(fetched)])
        copy.start()
        fetched.append(copy)
        return copy

    decay_in = fetch(decay_hbm, decay)
    load_cut = [
        fetch(load_hbm.at[1, :, :FACE], load.at[1, :, :FACE]),
        fetch(load_hbm.at[:, SY - 1, FACE:], load.at[:, SY - 1, FACE:]),
    ]
    small_in = [fetch(order_hbm, order), fetch(weight_hbm, weight)]
    load_rest = [
        fetch(load_hbm.at[0, :, :FACE], load.at[0, :, :FACE]),
        fetch(load_hbm.at[:, : SY - 1, FACE:], load.at[:, : SY - 1, FACE:]),
    ]
    inverse_in = fetch(inverse_hbm, blocks_p)
    schur_in = fetch(schur_hbm, blocks_s)

    sent = []

    def send(src, dst, peer):
        k = len(sent)
        copy = pltpu.make_async_remote_copy(
            src_ref=src, dst_ref=dst, send_sem=send_sem.at[k], recv_sem=recv_sem.at[k],
            device_id=peer, device_id_type=MESH,
        )
        copy.start()
        sent.append(copy)
        return copy

    def arrived(copies):
        for copy in copies:
            copy.wait_recv()

    east_open = (gx < nx - 1).astype(F32)
    west_open = (gx > 0).astype(F32)
    north_open = (gy < ng - 1).astype(F32)
    south_open = (gy > 0).astype(F32)

    decay_in.wait()
    ksrc[...] = jnp.zeros((SX, LANES), F32)
    ksrc[:, 0:SY] = jnp.exp(-decay[...])
    kz[z] = ksrc[...]
    for copy in load_cut:
        copy.wait()
    for b in range(SY):
        face = load[1, b, :FACE] * east_open
        load[1, b, :FACE] = face
        edge_w[0, 2, b] = face.astype(BF16)
    for a in range(SX):
        face = load[a, SY - 1, FACE:] * north_open
        load[a, SY - 1, FACE:] = face
        north_w[0, a, SY] = face.astype(BF16)
    pl.semaphore_wait(barrier, len(greeted))
    gather_k = [send(ksrc, kz.at[z], peer) for peer in z_peers]
    halo_n = [send(north_w.at[0, :, SY], north_w.at[0, :, 0], north)]
    halo_e = {
        b + CUT - 1: [send(edge_w.at[0, 2, b : b + CUT], edge_w.at[0, 0, b : b + CUT], east)]
        for b in range(SY - CUT, -1, -CUT)
    }

    for copy in small_in + load_rest:
        copy.wait()
    wcol[...] = jnp.transpose(jnp.broadcast_to(weight[...], (LANES, 2 * FACE)))
    w_east, w_north = wcol[:FACE], wcol[FACE:]

    def weigh(face, weights):
        value = [jnp.sum(face[:, h * LANES : (h + 1) * LANES] * weights, axis=0, keepdims=True) for h in range(2)]
        return jnp.concatenate(value, axis=0)

    def gather_ring(turn, rows):
        za[turn, z, 0:rows] = zsrc[turn, 0:rows]
        copies = []
        if turn:
            copies += [send(south_part, zs.at[z], peer) for peer in zs_peers]
        copies += [send(zsrc.at[turn, 0:rows], za.at[turn, z, 0:rows], peer) for peer in z_peers]
        return copies

    for a in range(SX):
        for b in range(SY):
            rows = slice(2 * b, 2 * b + 2)
            zsrc[0, a, rows] = weigh(load[a, b, :FACE], w_east) + weigh(load[a, b, FACE:], w_north)
    gather_z = gather_ring(0, SX)

    for b in range(SY):
        edge_w[0, 1, b] = load[0, b, :FACE].astype(BF16)
    for a in range(SX):
        for b in range(SY - 1):
            north_w[0, a, b + 1] = load[a, b, FACE:].astype(BF16)

    def fold_order(blocks):
        row = lax.broadcasted_iota(jnp.int32, (2 * FACE, 2 * FACE), 0)
        for a in range(SX):
            for b in range(SY):
                own = order[a, b]
                place = jnp.concatenate([own[0:1], own[1:2] + FACE], axis=1)
                hot_t = (row == jnp.broadcast_to(place, (2 * FACE, 2 * FACE))).astype(F32).astype(BF16)
                columns = lax.dot_general(
                    blocks[a, b, :, 2 * FACE :], hot_t, (((1,), (1,)), ((), ())), preferred_element_type=F32
                )
                blocks[a, b, :, 2 * FACE :] = columns.astype(BF16)
                rows = jnp.dot(hot_t, blocks[a, b, 2 * FACE :, :], preferred_element_type=F32)
                blocks[a, b, 2 * FACE :, :] = rows.astype(BF16)

    inverse_in.wait()
    fold_order(blocks_p)

    def group_keep():
        for r in range(group):
            for b in range(SY):
                rate = kz[r // SX, r % SX : r % SX + 1, b : b + 1]
                k_all[r, 2 * b : 2 * b + 2] = jnp.broadcast_to(rate, (2, LANES))
        product = jnp.ones((TILE, LANES), F32)
        squares = jnp.zeros((TILE, LANES), F32)
        for r in range(group):
            product = product * k_all[r]
            trans[r] = product
            squares = squares + product * product
        kw[0] = product
        kw[1] = squares
        ykw[y] = kw[...]
        return [send(kw, ykw.at[y], peer) for peer in y_peers]

    def group_solve(turn):
        for r in range(group):
            s, a = r // SX, r % SX
            if turn == 0:
                d_all[turn, r] = za[0, s, a]
            else:
                own = za[1, s, a + 1]
                if a == SX - 1 and s + 1 < nz:
                    own = own + za[1, s + 1, 0]
                d_all[turn, r] = own
                d_all[turn, r, 6:8] = d_all[turn, r, 6:8] + zs[s, a]
        climb = jnp.zeros((TILE, LANES), F32)
        for r in range(group):
            climb = k_all[r] * climb + d_all[turn, r]
            climb_l[turn, r] = climb
        back = jnp.zeros((TILE, LANES), F32)
        for r in range(group - 1, -1, -1):
            back = k_all[r] * (back + climb_l[turn, r])
        fg[turn, 0] = climb
        fg[turn, 1] = back
        if turn:
            fg[turn, 2] = za[1, 0, 0]
        count = 2 + turn
        ybuf[turn, y, 0:count] = fg[turn, 0:count]
        return [send(fg.at[turn, 0:count], ybuf.at[turn, y, 0:count], peer) for peer in y_peers]

    pending = {}

    def line_finish(turn):
        climb_in = jnp.zeros((TILE, LANES), F32)
        for j in range(ny):
            line_in[0, j] = climb_in
            climb_in = ykw[j, 0] * climb_in + ybuf[turn, j, 0]
            if turn:
                climb_in = climb_in + ybuf[1, (j + 1) % ny, 2]
        back = jnp.zeros((TILE, LANES), F32)
        for j in range(ny - 1, -1, -1):
            line_in[1, j] = back
            if turn:
                back = back + ybuf[1, (j + 1) % ny, 2]
            back = ykw[j, 0] * back + ybuf[turn, j, 1] + ykw[j, 1] * line_in[0, j]
            line_in[2, j] = back
        climb_in = line_in[0, y]
        back = line_in[1, y]
        if turn:
            handed = ybuf[1, (y + 1) % ny, 2]
            back = back + handed
            d_all[turn, group - 1] = d_all[turn, group - 1] + handed
        for r in range(group - 1, -1, -1):
            total = climb_l[turn, r] + trans[r] * climb_in + back
            settled_grp[turn, r + 1] = total
            back = k_all[r] * total
        settled_grp[turn, 0] = climb_in + line_in[2, y]
        total = jnp.zeros((8, LANES), F32)
        for r in range(SX + 1):
            value = settled_grp[turn, SX * z + r]
            settled[turn, r] = value
            if r == SX:
                pending["column"] = [send(settled.at[turn, 1:3, 6:8], ghost_col.at[turn], north)]
            if r:
                total = total + value[0:8] * d_all[turn, SX * z + r - 1, 0:8]
        return total[0:2] + total[2:4] + total[4:6] + total[6:8]

    def edge_sum(turn, r, b):
        if r == 0:
            return (acc_e[turn % 2, 0, b] + recv_e[turn, 0, b].astype(F32)) * west_open
        if r == SX:
            return (acc_e[turn % 2, 2, b] + recv_e[turn, 1, b].astype(F32)) * east_open
        return acc_e[turn % 2, r, b]

    def north_sum(turn, a, c):
        if c == 0:
            return (acc_n[turn % 2, a, 0] + recv_n[turn, 0, a].astype(F32)) * south_open
        if c == SY:
            return (acc_n[turn % 2, a, SY] + recv_n[turn, 1, a].astype(F32)) * north_open
        return acc_n[turn % 2, a, c]

    def spread(weights, pair):
        return jnp.concatenate([weights * pair[0:1], weights * pair[1:2]], axis=1)

    def edge_face(turn, coarse, out, r, b):
        value = edge_sum(turn, r, b)
        if coarse is not None:
            part = spread(w_east, settled[coarse, r, 2 * b : 2 * b + 2])
            if r == 0:
                part = part * west_open
            if r == SX:
                part = part * east_open
            value = 0.25 * value + part
            if r > 0:
                out[r - 1, b, :FACE] = value
        edge_w[turn + 1, r, b] = value.astype(BF16)

    def north_face(turn, coarse, out, a, c):
        value = north_sum(turn, a, c)
        if coarse is not None:
            pair = settled[coarse, a + 1, 2 * c - 2 : 2 * c] if c else ghost_col[coarse, a]
            part = spread(w_north, pair)
            if c == 0:
                part = part * south_open
            if c == SY:
                part = part * north_open
            value = 0.25 * value + part
            if c > 0:
                out[a, c - 1, FACE:] = value
        north_w[turn + 1, a, c] = value.astype(BF16)

    def stage(turn, blocks, halo_e, halo_n, coarse=None, out=None, between=None):
        if turn > 0:
            for b in range(SY):
                edge_face(turn - 1, coarse, out, 1, b)
            for a in range(SX):
                for c in range(1, SY):
                    north_face(turn - 1, coarse, out, a, c)
        now = turn % 2
        total = jnp.zeros((8, CASES), F32)
        next_e, next_n = {}, []
        for place, b in enumerate(ORDER):
            if between is not None and place == between[0]:
                between[1]()
            if turn == 0:
                if b == 0:
                    arrived(halo_n)
            elif b == SY - 1:
                arrived(halo_n[1])
                for a in range(SX):
                    north_face(turn - 1, coarse, out, a, SY)
            elif b == 0:
                arrived(halo_n[0])
                if coarse is not None:
                    arrived(pending["column"])
                for a in range(SX):
                    north_face(turn - 1, coarse, out, a, 0)
            if b in halo_e:
                arrived(halo_e[b])
            if turn > 0:
                edge_face(turn - 1, coarse, out, 2, b)
                edge_face(turn - 1, coarse, out, 0, b)
            for a in (1, 0):
                field = jnp.concatenate(
                    [edge_w[turn, a + 1, b], north_w[turn, a, b + 1], edge_w[turn, a, b], north_w[turn, a, b]], axis=0
                )
                image = jnp.dot(blocks[a, b], field, preferred_element_type=F32)
                total = total + jnp.sum((image * field.astype(F32)).reshape(4 * FACE // 8, 8, CASES), axis=0)
                if turn == 3:
                    continue
                img_e, img_n = image[:FACE], image[FACE : 2 * FACE]
                img_w, img_s = image[2 * FACE : 3 * FACE], image[3 * FACE :]
                if a == 1:
                    acc_e[now, 2, b] = img_e
                    send_e[turn, 0, b] = img_e.astype(BF16)
                    acc_e[now, 1, b] = img_w
                else:
                    acc_e[now, 1, b] = acc_e[now, 1, b] + img_e
                    acc_e[now, 0, b] = img_w
                    send_e[turn, 1, b] = img_w.astype(BF16)
                if b == SY - 1:
                    acc_n[now, a, b + 1] = img_n
                else:
                    acc_n[now, a, b + 1] = acc_n[now, a, b + 1] + img_n
                acc_n[now, a, b] = img_s
                if b == 0:
                    send_n[turn, 1, a] = img_s.astype(BF16)
                if b == SY - 1:
                    send_n[turn, 0, a] = img_n.astype(BF16)
            if turn == 3:
                continue
            if b % CUT == 0:
                some = slice(b, b + CUT)
                next_e[b + CUT - 1] = [
                    send(send_e.at[turn, 0, some], recv_e.at[turn, 0, some], east),
                    send(send_e.at[turn, 1, some], recv_e.at[turn, 1, some], west),
                ]
            if b == SY - 1:
                to_north = send(send_n.at[turn, 0], recv_n.at[turn, 0], north)
            if b == 0:
                to_south = send(send_n.at[turn, 1], recv_n.at[turn, 1], south)
        if turn < 3:
            next_n = [[to_north], [to_south]]
        if between is not None and between[0] == SY:
            between[1]()
        return total, next_e, next_n

    def by_half(total):
        whole = jnp.sum(total, axis=0, keepdims=True)
        return jnp.concatenate([whole[:, :LANES], whole[:, LANES:]], axis=0)

    def all_sum(source, middle, buf_a, buf_b):
        def first():
            buf_a[2 * z + core] = source[...]
            return [send(source, buf_a.at[2 * z + core], peer) for peer in a_peers]

        def second(copies):
            arrived(copies)
            value = buf_a[0]
            for k in range(1, 2 * nz):
                value = value + buf_a[k]
            middle[...] = value
            buf_b[nc * y + x] = value
            return [send(middle, buf_b.at[nc * y + x], peer) for peer in b_peers]

        def third(copies):
            arrived(copies)
            value = buf_b[0]
            for k in range(1, ny * nc):
                value = value + buf_b[k]
            return value

        return first, second, third

    def solve_ring(turn, copies):
        def run():
            if turn == 0:
                arrived(gather_k)
                pending["keep"] = group_keep()
            arrived(copies)
            pending[turn] = group_solve(turn)

        return run

    total0, halo_e, halo_n = stage(0, blocks_p, halo_e, halo_n, between=(PLACE0, solve_ring(0, gather_z)))
    schur_in.wait()
    fold_order(blocks_s)
    arrived(pending["keep"])
    arrived(pending[0])
    coarse0 = line_finish(0)
    total1, halo_e, halo_n = stage(1, blocks_s, halo_e, halo_n, 0, s_out)

    for b in range(SY):
        rows = slice(2 * b, 2 * b + 2)
        zsrc[1, 0, rows] = weigh(acc_e[1, 0, b], w_east) * west_open
        for a in range(SX):
            part_e, part_n = weigh(acc_e[1, a + 1, b], w_east), weigh(acc_n[1, a, b + 1], w_north)
            if a == SX - 1:
                part_e = part_e * east_open
            if b == SY - 1:
                part_n = part_n * north_open
            zsrc[1, a + 1, rows] = part_e + part_n
    for a in range(SX):
        south_part[a] = weigh(acc_n[1, a, 0], w_north) * south_open
    gather_z = gather_ring(1, SX + 1)

    mom[0:2] = 0.25 * by_half(total0) + coarse0
    mom[2:4] = by_half(total1)
    mom[6:8] = jnp.zeros((2, LANES), F32)

    total2, halo_e, halo_n = stage(2, blocks_p, halo_e, halo_n, between=(PLACE1, solve_ring(1, gather_z)))
    arrived(pending[1])
    coarse1 = line_finish(1)
    mom[4:6] = 0.25 * by_half(total2) + coarse1
    early = all_sum(mom, mid, sum_a, sum_b)
    early_a = early[0]()

    total3, _, _ = stage(3, blocks_s, halo_e, halo_n, 1, t_out)
    mom3[...] = by_half(total3)
    late = all_sum(mom3, mid3, sum3_a, sum3_b)
    late_a = late[0]()
    early_b = early[1](early_a)
    late_b = late[1](late_a)
    reduced = early[2](early_b)
    m3 = late[2](late_b)
    m0, m1, m2 = reduced[0:2], reduced[2:4], reduced[4:6]
    step0 = m0 / m1
    inner1 = step0 * step0 * m2 - m0
    beta = inner1 / m0
    mixed = m1 - step0 * m2
    curvature1 = mixed - step0 * m2 + step0 * step0 * m3 + 2.0 * beta * mixed + beta * beta * m1
    step1 = inner1 / curvature1
    first, second = step0 + step1 * (1.0 + beta), -step0 * step1
    first = jnp.concatenate([first[0:1], first[1:2]], axis=1)
    second = jnp.concatenate([second[0:1], second[1:2]], axis=1)
    written = []
    for a in range(SX):
        for b in range(0, SY, 2):
            for c in (b, b + 1):
                s_out[a, c] = first * s_out[a, c] + second * t_out[a, c]
            written.append(fetch(s_out.at[a, b : b + 2], x_hbm.at[a, b : b + 2]))

    for copy in written:
        copy.wait()
    for copy in sent:
        copy.wait_send()


def local(mesh_sizes, load_field, schur_blocks, local_inverse, face_order, coarse_weights, coarse_decay):
    ny, nz, ng = mesh_sizes
    nc, group = ng // 2, SX * nz
    n_sends = 1 + 3 * 2 + 7 * (SY // CUT) + 3 * (nz - 1 + ny - 1) + nz + 2 + 2 * (2 * nz - 1 + ny * nc - 1)
    field = (SX, SY, 2 * FACE, CASES)
    return pl.pallas_call(
        functools.partial(kernel, ny, nz, ng),
        out_shape=jax.ShapeDtypeStruct(field, F32),
        in_specs=[pl.BlockSpec(memory_space=pltpu.HBM)] * 6,
        out_specs=pl.BlockSpec(memory_space=pltpu.HBM),
        scratch_shapes=[
            pltpu.VMEM(field, F32),
            pltpu.VMEM(field, F32),
            pltpu.VMEM(field, F32),
            pltpu.VMEM((SX, SY, 4 * FACE, 4 * FACE), BF16),
            pltpu.VMEM((SX, SY, 4 * FACE, 4 * FACE), BF16),
            pltpu.VMEM((SX, SY, 2, FACE), jnp.int32),
            pltpu.VMEM((1, 2 * FACE), F32),
            pltpu.VMEM((SX, SY), F32),
            pltpu.VMEM((2 * FACE, LANES), F32),
            pltpu.VMEM((4, SX + 1, SY, FACE, CASES), BF16),
            pltpu.VMEM((4, SX, SY + 1, FACE, CASES), BF16),
            pltpu.VMEM((2, SX + 1, SY, FACE, CASES), F32),
            pltpu.VMEM((2, SX, SY + 1, FACE, CASES), F32),
            pltpu.VMEM((3, 2, SY, FACE, CASES), BF16),
            pltpu.VMEM((3, 2, SX, FACE, CASES), BF16),
            pltpu.VMEM((3, 2, SY, FACE, CASES), BF16),
            pltpu.VMEM((3, 2, SX, FACE, CASES), BF16),
            pltpu.VMEM((SX, LANES), F32),
            pltpu.VMEM((nz, SX, LANES), F32),
            pltpu.VMEM((2, TILE, LANES), F32),
            pltpu.VMEM((ny, 2, TILE, LANES), F32),
            pltpu.VMEM((2, SX + 1, TILE, LANES), F32),
            pltpu.VMEM((2, nz, SX + 1, TILE, LANES), F32),
            pltpu.VMEM((nz, SX, 2, LANES), F32),
            pltpu.VMEM((SX, 2, LANES), F32),
            pltpu.VMEM((2, group, TILE, LANES), F32),
            pltpu.VMEM((group, TILE, LANES), F32),
            pltpu.VMEM((2, group, TILE, LANES), F32),
            pltpu.VMEM((group, TILE, LANES), F32),
            pltpu.VMEM((2, 3, TILE, LANES), F32),
            pltpu.VMEM((2, ny, 3, TILE, LANES), F32),
            pltpu.VMEM((3, ny, TILE, LANES), F32),
            pltpu.VMEM((2, group + 1, TILE, LANES), F32),
            pltpu.VMEM((2, SX + 1, TILE, LANES), F32),
            pltpu.VMEM((2, SX, 2, LANES), F32),
            pltpu.VMEM((8, LANES), F32),
            pltpu.VMEM((8, LANES), F32),
            pltpu.VMEM((2 * nz, 8, LANES), F32),
            pltpu.VMEM((ny * nc, 8, LANES), F32),
            pltpu.VMEM((2, LANES), F32),
            pltpu.VMEM((2, LANES), F32),
            pltpu.VMEM((2 * nz, 2, LANES), F32),
            pltpu.VMEM((ny * nc, 2, LANES), F32),
            pltpu.SemaphoreType.DMA((13,)),
            pltpu.SemaphoreType.DMA((n_sends,)),
            pltpu.SemaphoreType.DMA((n_sends,)),
        ],
        compiler_params=pltpu.CompilerParams(
            collective_id=0, has_side_effects=True, vmem_limit_bytes=60 << 20
        ),
        cost_estimate=pl.CostEstimate(flops=1_100_000_000, bytes_accessed=6 << 20, transcendentals=8),
    )(load_field, schur_blocks, local_inverse, face_order, coarse_weights.reshape(1, -1), coarse_decay)


def solution(mesh):
    nx, ng = mesh.shape["gx"], mesh.shape["gy"]
    nz = 8 if nx % 8 == 0 else 2
    in_specs = (
        P("gx", "gy", None, None),
        P("gx", "gy", None, None),
        P("gx", "gy", None, None),
        P("gx", "gy", None, None),
        P(),
        P("gx", "gy"),
    )
    return jax.shard_map(
        functools.partial(local, (nx // nz, nz, ng)),
        mesh=mesh, in_specs=in_specs, out_specs=P("gx", "gy", None, None), check_vma=False,
    )
```
